32 devices in a mesh: grp: 2 (over y), col: 4 (over z), row: 4 (over x, core).
Axes of the slice: x: 2, y: 2, z: 4, core: 2. Of those that a mesh axis runs over, the one named last changes fastest.
Arguments:
- spectra: bfloat16 [2, 8, 256, 2048], P(None, None, ('grp', 'col'), 'row'), parts along dimension 2, may hold values from -6 to 6
- pair_mask: int32 [8, 4], P('grp', 'col'), parts along dimension 0, may hold values from 0 to 1, as said below
Outputs:
- correlations: bfloat16 [32, 4, 256, 1024], P('row', None, ('grp', 'col')), parts along dimension 2
The draws below stay inside these ranges and needn't reach their ends.
There are 2 independent parts, one for each index of `grp`. The reference program is written for one: setup_inputs(seed, part) draws one part's arguments, and reference() takes and returns one part's arrays. A program takes and returns all parts, laid end to end along the dimension named above; each array names one. Nothing has to cross between parts.
Inputs may be any that keep to these rules, and one draw needn't show every extreme that they name: pair_mask[k, b] is 0 wherever b + k >= 4.
All inputs are finite; a program needn't handle non-finite values.
Results may differ from the reference program's by a relative error of at most 0.0033.
Values may be sent and summed in bfloat16 or wider, within the bound.
A program may use at most 128 MiB of HBM per device.

```python
import math
import jax
import jax.numpy as jnp

CB = 32
WIN = 8
F = 2048
L = 1024
NFFT = 65536
LO_BIN = 2048
K = 4
NBLK = 4
C = 128


def draw_pair_mask(key, part):
    key = jax.random.fold_in(key, 7)
    picks = jax.random.randint(key, (K, NBLK), 0, 10)
    valid = jnp.arange(NBLK)[None, :] + jnp.arange(K)[:, None] < NBLK
    return ((picks < 7) & valid).astype(jnp.int32)


def levels(rng, extent, shards, low, top_value):
    loudness, own = 1.0, jax.random.fold_in(rng, 6)
    for dim, parts in shards:
        draws = jnp.exp(jax.random.uniform(jax.random.fold_in(own, dim), (parts,), jnp.float32, low / len(shards), top_value / len(shards)))
        loudness = loudness * jnp.repeat(draws, extent[dim] // parts).reshape([-1 if axis == dim else 1 for axis in range(len(extent))])
    return loudness


def bell_draw(own_key, extent, width, limit, split=(), kind=jnp.bfloat16):
    factor_of = levels(own_key, extent, split, -0.22, 0.18) if split else 1.0
    entries = jax.random.normal(own_key, extent, jnp.float32) * width * factor_of
    return jnp.minimum(jnp.maximum(entries, -limit), limit).astype(kind)


def setup_inputs(seed: int = 0, part: int = 0) -> dict:
    splits = jax.random.split(jax.random.key(seed), 3)
    part_splits = jax.random.split(jax.random.fold_in(splits[2], part), 3)
    return {
        "spectra": bell_draw(part_splits[0], (2, WIN, C, F), 1.0, 6.0, ((2, 4), (3, 4))),
        "pair_mask": draw_pair_mask(jax.random.fold_in(jax.random.fold_in(splits[2], part), 71), part),
    }


def make_tables():
    bins = LO_BIN + jnp.arange(F, dtype=jnp.int32)
    lags = jnp.arange(L, dtype=jnp.int32) - L // 2
    turns = jnp.mod(bins[:, None] * lags[None, :], NFFT).astype(jnp.float32)
    phase = turns * (2.0 * math.pi / NFFT)
    return (jnp.cos(phase).astype(jnp.bfloat16), jnp.sin(phase).astype(jnp.bfloat16))

def reference(spectra, pair_mask):
    real_part = spectra[0].astype(jnp.float32)
    imag_part = spectra[1].astype(jnp.float32)
    magnitude = jnp.sqrt(real_part * real_part + imag_part * imag_part)
    denom = jnp.maximum(magnitude, 0.5)
    white = (spectra.astype(jnp.float32) / denom[None]).astype(jnp.bfloat16)
    blocks = white.reshape(2, WIN, NBLK, CB, F)
    cos_table, sin_table = make_tables()
    scale = 1.0 / math.sqrt(F * WIN)
    results = []
    for offset in range(K):
        pad = jnp.zeros((2, WIN, offset, CB, F), white.dtype)
        partner = jnp.concatenate([blocks[:, :, offset:], pad], axis=2)
        owner_f = blocks.astype(jnp.float32)
        partner_f = partner.astype(jnp.float32)
        cross_real = jnp.einsum('wbif,wbjf->jbif', owner_f[0], partner_f[0]) + jnp.einsum('wbif,wbjf->jbif', owner_f[1], partner_f[1])
        cross_imag = jnp.einsum('wbif,wbjf->jbif', owner_f[0], partner_f[1]) - jnp.einsum('wbif,wbjf->jbif', owner_f[1], partner_f[0])
        keep = pair_mask[offset].astype(jnp.float32)[None, :, None, None]
        cross_real = (cross_real * keep).astype(jnp.bfloat16).reshape(-1, F)
        cross_imag = (cross_imag * keep).astype(jnp.bfloat16).reshape(-1, F)
        lagged = jnp.dot(cross_real, cos_table, preferred_element_type=jnp.float32) - jnp.dot(cross_imag, sin_table, preferred_element_type=jnp.float32)
        results.append((lagged * scale).astype(jnp.bfloat16).reshape(CB, NBLK * CB, L))
    return jnp.stack(results, axis=1)
```

```python
import functools
import math

import jax
import jax.numpy as jnp
import numpy as np
from jax import lax
from jax.experimental import pallas as pl
from jax.experimental.pallas import tpu as pltpu
from jax.sharding import PartitionSpec as P

WIN = 8
F = 2048
L = 1024
NFFT = 65536
LO_BIN = 2048
GROUP = 8
ROWS = WIN * GROUP
LANES = 128
MESH = pl.DeviceIdType.MESH


def lag_tables(shards):
    bins = LO_BIN + np.arange(F, dtype=np.int32)
    lags = np.arange(L, dtype=np.int32) - L // 2
    turns = np.mod(bins[:, None] * lags[None, :], NFFT).astype(np.float32)
    phase = (turns * np.float32(2.0 * math.pi / NFFT)).astype(np.float64)
    parts = [
        part.astype(np.float32).astype(jnp.bfloat16).reshape(shards, F // shards, L)
        for part in (np.cos(phase), -np.sin(phase))
    ]
    return np.concatenate(parts, axis=1)


def xor(index, mask):
    result = index
    bit = 1
    while bit <= mask:
        if mask & bit:
            result = result + bit - 2 * bit * lax.rem(lax.div(index, bit), 2)
        bit *= 2
    return result


def schedule(shards, offsets):
    far = range(2, shards)
    events = [("T", 0, 1), ("X", 0, 0), ("T", 0, 2), ("O", 1), ("X", 0, 1)]
    events += [("T", 0, m) for m in far if m > 2]
    events += [("T", 1, 0), ("X", 1, 0), ("T", 1, 1), ("X", 1, 1)]
    events += [("T", 1, m) for m in far]
    events += [("T", 2, 0), ("X", 2, 0), ("O", 2), ("O", 3), ("X", 0, 2), ("T", 2, 1), ("X", 0, 3)]
    events += [("X", 1, 2), ("T", 2, 2), ("X", 1, 3), ("T", 2, 3), ("X", 2, 1), ("T", 3, 0), ("X", 2, 2)]
    events += [("X", 2, 3), ("T", 3, 1), ("X", 3, 0), ("T", 3, 2), ("X", 3, 1), ("X", 3, 2)]
    events += [("T", 3, 3), ("X", 3, 3)]
    for m in range(4, shards):
        events += [("O", m), ("T", 2, m), ("T", 3, m)]
        events += [("X", k, m) for k in range(offsets)]
    return events


def kernel(
    shards, blocks, offsets, spectra, mask, table_hbm, out,
    owner, partner, table, products, total, sums,
    table_sem, o_send, o_recv, t_send, t_recv, z_send, z_recv,
):
    me = lax.axis_index("row")
    block = lax.axis_index("col")
    bins = spectra.shape[3]
    groups = owner.shape[1]
    mine = groups * GROUP // shards
    left = lax.rem(block + blocks - 1, blocks)
    right = lax.rem(block + 1, blocks)

    load = pltpu.make_async_copy(table_hbm, table, table_sem)
    load.start()

    barrier = pltpu.get_barrier_semaphore()
    for m in range(1, shards):
        pl.semaphore_signal(barrier, inc=1, device_id={"row": xor(me, m)}, device_id_type=MESH)

    @pl.when(block > 0)
    def _():
        pl.semaphore_signal(barrier, inc=1, device_id={"col": left}, device_id_type=MESH)

    @pl.when(block < blocks - 1)
    def _():
        pl.semaphore_signal(barrier, inc=1, device_id={"col": right}, device_id_type=MESH)

    def whiten(step, carry):
        lanes = pl.ds(pl.multiple_of(step * LANES, LANES), LANES)
        for pair in range(WIN // 2):
            parts = []
            for w in (2 * pair, 2 * pair + 1):
                re = spectra[0, w, :, lanes].astype(jnp.float32)
                im = spectra[1, w, :, lanes].astype(jnp.float32)
                denom = jnp.maximum(jnp.sqrt(re * re + im * im), 0.5)
                parts.append((re / denom, im / denom))
            for c in range(2):
                for g in range(groups):
                    rows = slice(g * GROUP, (g + 1) * GROUP)
                    both = jnp.concatenate([parts[0][c][rows], parts[1][c][rows]], axis=0)
                    owner[0, g, pl.ds(c * ROWS + pair * 2 * GROUP, 2 * GROUP), lanes] = both.astype(jnp.bfloat16)
        return carry

    lax.fori_loop(0, bins // LANES, whiten, 0)

    def group_of(row):
        return lax.div(row * mine, GROUP)

    partner[0, 0] = owner[0, group_of(me)]

    inner = (block > 0).astype(jnp.int32) + (block < blocks - 1).astype(jnp.int32)
    pl.semaphore_wait(barrier, inner + (shards - 1))

    def z_copy(k, m):
        return pltpu.make_async_remote_copy(
            src_ref=partner.at[k - 1, m], dst_ref=partner.at[k, m],
            send_sem=z_send.at[k - 1, m], recv_sem=z_recv.at[k - 1, m],
            device_id={"col": left}, device_id_type=MESH,
        )

    def t_copy(m):
        peer = xor(me, m)
        return pltpu.make_async_remote_copy(
            src_ref=owner.at[0, group_of(peer)], dst_ref=partner.at[0, m],
            send_sem=t_send.at[m], recv_sem=t_recv.at[m],
            device_id={"row": peer}, device_id_type=MESH,
        )

    def o_copy(m):
        relayed = m % 2 == 1 and m > 1
        return pltpu.make_async_remote_copy(
            src_ref=owner.at[m - 1 if relayed else 0], dst_ref=owner.at[m],
            send_sem=o_send.at[m], recv_sem=o_recv.at[m],
            device_id={"row": xor(me, 1 if relayed else m)}, device_id_type=MESH,
        )

    def forward(k, m):
        if k < offsets:
            @pl.when((block > 0) & (block + k - 1 < blocks))
            def _():
                z_copy(k, m).start()

    forward(1, 0)
    for m in range(1, shards):
        t_copy(m).start()
    o_copy(1).start()
    for m in range(2, shards, 2):
        o_copy(m).start()
    load.wait()

    first_row = lax.rem(me * mine, GROUP) if mine < GROUP else 0

    def correlate(k, m):
        chunk = xor(me, m)
        re = partner[k, m, :ROWS, :].astype(jnp.float32)
        im = partner[k, m, ROWS:, :].astype(jnp.float32)
        for number, rows in enumerate((re, re + im, im - re)):
            kept = rows
            for offset in range(mine, GROUP, mine):
                moved = jnp.concatenate([rows[offset:], rows[:offset]], axis=0)
                kept = jnp.where(first_row == offset, moved, kept)
            sums[number] = kept
        steps = bins // LANES

        def tile(step, carry):
            g = lax.div(step, steps)
            at = pl.multiple_of(lax.rem(step, steps) * LANES, LANES)
            lanes = pl.ds(at, LANES)
            a = owner[m, g, :ROWS, lanes].astype(jnp.float32)
            b = owner[m, g, ROWS:, lanes].astype(jnp.float32)
            a = [a[w * GROUP:(w + 1) * GROUP] for w in range(WIN)]
            b = [b[w * GROUP:(w + 1) * GROUP] for w in range(WIN)]
            p = [x - y for x, y in zip(a, b)]
            for pair in range(mine // 2):
                reals, imags = [], []
                for j in (2 * pair, 2 * pair + 1):
                    s = [None, None, None]
                    for w in range(WIN):
                        row = pl.ds(w * GROUP + j, 1)
                        terms = (
                            p[w] * sums[0, row, lanes],
                            b[w] * sums[1, row, lanes],
                            a[w] * sums[2, row, lanes],
                        )
                        s = [t if x is None else x + t for x, t in zip(s, terms)]
                    reals.append(s[0] + s[1])
                    imags.append(s[0] + s[2])
                rows = pl.ds(pl.multiple_of(g * (mine * GROUP) + pair * 2 * GROUP, 2 * GROUP), 2 * GROUP)
                products[rows, lanes] = jnp.concatenate(reals, axis=0).astype(jnp.bfloat16)
                products[rows, pl.ds(at + bins, LANES)] = jnp.concatenate(imags, axis=0).astype(jnp.bfloat16)
            return carry

        lax.fori_loop(0, groups * steps, tile, 0)
        wide = 256

        def lags(step, carry):
            columns = pl.ds(pl.multiple_of(step * wide, wide), wide)
            part = jnp.dot(products[...], table[chunk, :, columns], preferred_element_type=jnp.float32)
            if m > 0:
                part = part + total[k, :, columns]
            total[k, :, columns] = part
            return carry

        lax.fori_loop(0, L // wide, lags, 0)

    def finish(k):
        factor = mask[k, 0].astype(jnp.float32) * (1.0 / math.sqrt(F * WIN))
        for j in range(mine):
            for g in range(0, groups, 2):
                pieces = [total[k, pl.ds(((g + s) * mine + j) * GROUP, GROUP), :] for s in range(2)]
                both = jnp.concatenate(pieces, axis=0) * factor
                out[j, k, pl.ds(g * GROUP, 2 * GROUP), :] = both.astype(out.dtype)

    done = [0] * offsets
    for event in schedule(shards, offsets):
        if event[0] == "O":
            m = event[1]
            o_copy(m).wait_recv()
            if m % 2 == 0:
                o_copy(m + 1).start()
        elif event[0] == "T":
            k, m = event[1:]
            if k == 0:
                t_copy(m).wait_recv()
            else:
                @pl.when(block + k < blocks)
                def _(k=k, m=m):
                    z_copy(k, m).wait_recv()
            forward(k + 1, m)
        else:
            k, m = event[1:]
            done[k] += 1

            @pl.when(block + k < blocks)
            def _(k=k, m=m):
                correlate(k, m)
                if done[k] == shards:
                    finish(k)

            if done[k] == shards and k > 0:
                @pl.when(block + k >= blocks)
                def _(k=k):
                    out[:, k] = jnp.zeros((mine, groups * GROUP, L), out.dtype)

    for m in range(1, shards):
        t_copy(m).wait_send()
        o_copy(m).wait_send()
    for k in range(1, offsets):
        @pl.when((block > 0) & (block + k - 1 < blocks))
        def _(k=k):
            for m in range(shards):
                z_copy(k, m).wait_send()


def body(shards, blocks, spectra, pair_mask):
    channels, bins = spectra.shape[2:]
    offsets = pair_mask.shape[0]
    groups = channels // GROUP
    mine = channels // shards
    table = lag_tables(shards)
    chunk = (2 * ROWS, bins)
    pairs = mine * channels
    dma = pltpu.SemaphoreType.DMA
    return pl.pallas_call(
        functools.partial(kernel, shards, blocks, offsets),
        out_shape=jax.ShapeDtypeStruct((mine, offsets, channels, L), jnp.bfloat16),
        in_specs=[
            pl.BlockSpec(memory_space=pltpu.VMEM),
            pl.BlockSpec(memory_space=pltpu.SMEM),
            pl.BlockSpec(memory_space=pl.ANY),
        ],
        out_specs=pl.BlockSpec(memory_space=pltpu.VMEM),
        scratch_shapes=[
            pltpu.VMEM((shards, groups) + chunk, jnp.bfloat16),
            pltpu.VMEM((offsets, shards) + chunk, jnp.bfloat16),
            pltpu.VMEM(table.shape, jnp.bfloat16),
            pltpu.VMEM((pairs, 2 * bins), jnp.bfloat16),
            pltpu.VMEM((offsets, pairs, L), jnp.float32),
            pltpu.VMEM((3, ROWS, bins), jnp.float32),
            dma,
            dma((shards,)),
            dma((shards,)),
            dma((shards,)),
            dma((shards,)),
            dma((offsets - 1, shards)),
            dma((offsets - 1, shards)),
        ],
        compiler_params=pltpu.CompilerParams(
            collective_id=0, has_side_effects=True, vmem_limit_bytes=48 * 1024 * 1024
        ),
    )(spectra, pair_mask, table)


def solution(mesh):
    return jax.shard_map(
        functools.partial(body, mesh.shape["row"], mesh.shape["col"]),
        mesh=mesh,
        in_specs=(P(None, None, ("grp", "col"), "row"), P("grp", "col")),
        out_specs=P("row", None, ("grp", "col"), None),
        check_vma=False,
    )
```

```python
import functools
import math

import jax
import jax.numpy as jnp
import numpy as np
from jax import lax
from jax.experimental import pallas as pl
from jax.experimental.pallas import tpu as pltpu
from jax.sharding import PartitionSpec as P

WIN = 8
F = 2048
L = 1024
NFFT = 65536
LO_BIN = 2048
GROUP = 8
ROWS = WIN * GROUP
LANES = 128
MESH = pl.DeviceIdType.MESH


def lag_tables(shards):
    bins = LO_BIN + np.arange(F, dtype=np.int32)
    lags = np.arange(L, dtype=np.int32) - L // 2
    turns = np.mod(bins[:, None] * lags[None, :], NFFT).astype(np.float32)
    phase = (turns * np.float32(2.0 * math.pi / NFFT)).astype(np.float64)
    parts = [
        part.astype(np.float32).astype(jnp.bfloat16).reshape(shards, F // shards, L)
        for part in (np.cos(phase), -np.sin(phase))
    ]
    return np.concatenate(parts, axis=1)


def xor(index, mask):
    result = index
    bit = 1
    while bit <= mask:
        if mask & bit:
            result = result + bit - 2 * bit * lax.rem(lax.div(index, bit), 2)
        bit *= 2
    return result


def schedule(shards, offsets):
    far = range(2, shards)
    events = [("T", 0, 1), ("X", 0, 0), ("T", 0, 2), ("O", 1), ("X", 0, 1)]
    events += [("T", 0, m) for m in far if m > 2]
    events += [("T", 1, 0), ("X", 1, 0), ("T", 1, 1), ("X", 1, 1)]
    events += [("T", 1, m) for m in far]
    events += [("T", 2, 0), ("X", 2, 0), ("O", 2), ("O", 3), ("X", 0, 2), ("T", 2, 1), ("X", 0, 3)]
    events += [("X", 1, 2), ("T", 2, 2), ("X", 1, 3), ("T", 2, 3), ("X", 2, 1), ("T", 3, 0), ("X", 2, 2)]
    events += [("X", 2, 3), ("T", 3, 1), ("X", 3, 0), ("T", 3, 2), ("X", 3, 1), ("X", 3, 2)]
    events += [("T", 3, 3), ("X", 3, 3)]
    for m in range(4, shards):
        events += [("O", m), ("T", 2, m), ("T", 3, m)]
        events += [("X", k, m) for k in range(offsets)]
    return events


def kernel(
    shards, blocks, offsets, spectra_hbm, mask, table_hbm, out,
    spectra, owner, partner, table, products, total, sums,
    spectra_sem, table_sem, o_send, o_recv, t_send, t_recv, z_send, z_recv,
):
    me = lax.axis_index("row")
    block = lax.axis_index("col")
    bins = spectra.shape[3]
    groups = owner.shape[1]
    mine = groups * GROUP // shards
    left = lax.rem(block + blocks - 1, blocks)
    right = lax.rem(block + 1, blocks)

    load = pltpu.make_async_copy(table_hbm, table, table_sem)
    fetch = pltpu.make_async_copy(spectra_hbm, spectra, spectra_sem)
    fetch.start()

    barrier = pltpu.get_barrier_semaphore()
    for m in range(1, shards):
        pl.semaphore_signal(barrier, inc=1, device_id={"row": xor(me, m)}, device_id_type=MESH)

    @pl.when(block > 0)
    def _():
        pl.semaphore_signal(barrier, inc=1, device_id={"col": left}, device_id_type=MESH)

    @pl.when(block < blocks - 1)
    def _():
        pl.semaphore_signal(barrier, inc=1, device_id={"col": right}, device_id_type=MESH)

    def whiten(step, carry):
        lanes = pl.ds(pl.multiple_of(step * LANES, LANES), LANES)
        for pair in range(WIN // 2):
            parts = []
            for w in (2 * pair, 2 * pair + 1):
                re = spectra[0, w, :, lanes].astype(jnp.float32)
                im = spectra[1, w, :, lanes].astype(jnp.float32)
                denom = jnp.maximum(jnp.sqrt(re * re + im * im), 0.5)
                parts.append((re / denom, im / denom))
            for c in range(2):
                for g in range(groups):
                    rows = slice(g * GROUP, (g + 1) * GROUP)
                    both = jnp.concatenate([parts[0][c][rows], parts[1][c][rows]], axis=0)
                    owner[0, g, pl.ds(c * ROWS + pair * 2 * GROUP, 2 * GROUP), lanes] = both.astype(jnp.bfloat16)
        return carry

    fetch.wait()
    load.start()
    lax.fori_loop(0, bins // LANES, whiten, 0)

    def group_of(row):
        return lax.div(row * mine, GROUP)

    partner[0, 0] = owner[0, group_of(me)]

    inner = (block > 0).astype(jnp.int32) + (block < blocks - 1).astype(jnp.int32)
    pl.semaphore_wait(barrier, inner + (shards - 1))

    def z_copy(k, m):
        return pltpu.make_async_remote_copy(
            src_ref=partner.at[k - 1, m], dst_ref=partner.at[k, m],
            send_sem=z_send.at[k - 1, m], recv_sem=z_recv.at[k - 1, m],
            device_id={"col": left}, device_id_type=MESH,
        )

    def t_copy(m):
        peer = xor(me, m)
        return pltpu.make_async_remote_copy(
            src_ref=owner.at[0, group_of(peer)], dst_ref=partner.at[0, m],
            send_sem=t_send.at[m], recv_sem=t_recv.at[m],
            device_id={"row": peer}, device_id_type=MESH,
        )

    def o_copy(m):
        relayed = m % 2 == 1 and m > 1
        return pltpu.make_async_remote_copy(
            src_ref=owner.at[m - 1 if relayed else 0], dst_ref=owner.at[m],
            send_sem=o_send.at[m], recv_sem=o_recv.at[m],
            device_id={"row": xor(me, 1 if relayed else m)}, device_id_type=MESH,
        )

    def forward(k, m):
        if k < offsets:
            @pl.when((block > 0) & (block + k - 1 < blocks))
            def _():
                z_copy(k, m).start()

    forward(1, 0)
    for m in range(1, shards):
        t_copy(m).start()
    o_copy(1).start()
    for m in range(2, shards, 2):
        o_copy(m).start()
    load.wait()

    first_row = lax.rem(me * mine, GROUP) if mine < GROUP else 0

    steps = bins // LANES
    wide = L // groups

    def prepare(k, m):
        re = partner[k, m, :ROWS, :].astype(jnp.float32)
        im = partner[k, m, ROWS:, :].astype(jnp.float32)
        for number, rows in enumerate((re, re + im, im - re)):
            kept = rows
            for offset in range(mine, GROUP, mine):
                moved = jnp.concatenate([rows[offset:], rows[:offset]], axis=0)
                kept = jnp.where(first_row == offset, moved, kept)
            sums[number] = kept

    def cross(m, slot, g, step):
        lanes = pl.ds(step * LANES, LANES)
        a = owner[m, g, :ROWS, lanes].astype(jnp.float32)
        b = owner[m, g, ROWS:, lanes].astype(jnp.float32)
        a = [a[w * GROUP:(w + 1) * GROUP] for w in range(WIN)]
        b = [b[w * GROUP:(w + 1) * GROUP] for w in range(WIN)]
        p = [x - y for x, y in zip(a, b)]
        for pair in range(mine // 2):
            reals, imags = [], []
            for j in (2 * pair, 2 * pair + 1):
                s = [None, None, None]
                for w in range(WIN):
                    row = pl.ds(w * GROUP + j, 1)
                    terms = (
                        p[w] * sums[0, row, lanes],
                        b[w] * sums[1, row, lanes],
                        a[w] * sums[2, row, lanes],
                    )
                    s = [t if x is None else x + t for x, t in zip(s, terms)]
                reals.append(s[0] + s[1])
                imags.append(s[0] + s[2])
            rows = pl.ds(pl.multiple_of(g * (mine * GROUP) + pair * 2 * GROUP, 2 * GROUP), 2 * GROUP)
            products[slot, rows, lanes] = jnp.concatenate(reals, axis=0).astype(jnp.bfloat16)
            products[slot, rows, pl.ds(bins + step * LANES, LANES)] = jnp.concatenate(imags, axis=0).astype(jnp.bfloat16)

    def lags(k, m, slot, g):
        columns = pl.ds(pl.multiple_of(g * wide, wide), wide)
        part = jnp.dot(products[slot], table[xor(me, m), :, columns], preferred_element_type=jnp.float32)
        if m > 0:
            part = part + total[k, :, columns]
        total[k, :, columns] = part

    def work(task, earlier):
        if task:
            prepare(*task[:2])

        def one(g, carry):
            if earlier:
                lags(*earlier, g)
            if task:
                for step in range(steps):
                    cross(task[1], task[2], g, step)
            return carry

        lax.fori_loop(0, groups, one, 0)
        if earlier and earlier[1] == shards - 1:
            finish(earlier[0])

    def finish(k):
        factor = mask[0, k].astype(jnp.float32) * (1.0 / math.sqrt(F * WIN))
        for j in range(mine):
            for g in range(0, groups, 2):
                pieces = [total[k, pl.ds(((g + s) * mine + j) * GROUP, GROUP), :] for s in range(2)]
                both = jnp.concatenate(pieces, axis=0) * factor
                out[j, k, pl.ds(g * GROUP, 2 * GROUP), :] = both.astype(out.dtype)

    def active(k):
        return block + k < blocks

    for k in range(1, offsets):
        @pl.when(block + k >= blocks)
        def _(k=k):
            out[:, k] = jnp.zeros((mine, groups * GROUP, L), out.dtype)

    pending, slot = None, 0
    for event in schedule(shards, offsets):
        if event[0] == "O":
            m = event[1]
            o_copy(m).wait_recv()
            if m % 2 == 0:
                o_copy(m + 1).start()
        elif event[0] == "T":
            k, m = event[1:]
            if k == 0:
                t_copy(m).wait_recv()
            else:
                @pl.when(block + k < blocks)
                def _(k=k, m=m):
                    z_copy(k, m).wait_recv()
            forward(k + 1, m)
        else:
            task = event[1:] + (slot,)
            k = task[0]
            older = pending[0] if pending else k

            @pl.when(active(max(k, older)))
            def _(task=task, pending=pending):
                work(task, pending)

            if older < k:
                @pl.when(active(older) & (block + k >= blocks))
                def _(pending=pending):
                    work(None, pending)

            if older > k:
                @pl.when(active(k) & (block + older >= blocks))
                def _(task=task):
                    work(task, None)

            pending, slot = task, 1 - slot

    @pl.when(active(pending[0]))
    def _():
        work(None, pending)

    for m in range(1, shards):
        t_copy(m).wait_send()
        o_copy(m).wait_send()
    for k in range(1, offsets):
        @pl.when((block > 0) & (block + k - 1 < blocks))
        def _(k=k):
            for m in range(shards):
                z_copy(k, m).wait_send()


def body(shards, blocks, spectra, pair_mask):
    channels, bins = spectra.shape[2:]
    offsets = pair_mask.shape[0]
    groups = channels // GROUP
    mine = channels // shards
    table = lag_tables(shards)
    chunk = (2 * ROWS, bins)
    pairs = mine * channels
    dma = pltpu.SemaphoreType.DMA
    return pl.pallas_call(
        functools.partial(kernel, shards, blocks, offsets),
        out_shape=jax.ShapeDtypeStruct((mine, offsets, channels, L), jnp.bfloat16),
        in_specs=[
            pl.BlockSpec(memory_space=pl.ANY),
            pl.BlockSpec(memory_space=pltpu.SMEM),
            pl.BlockSpec(memory_space=pl.ANY),
        ],
        out_specs=pl.BlockSpec(memory_space=pltpu.VMEM),
        scratch_shapes=[
            pltpu.VMEM(spectra.shape, jnp.bfloat16),
            pltpu.VMEM((shards, groups) + chunk, jnp.bfloat16),
            pltpu.VMEM((offsets, shards) + chunk, jnp.bfloat16),
            pltpu.VMEM(table.shape, jnp.bfloat16),
            pltpu.VMEM((2, pairs, 2 * bins), jnp.bfloat16),
            pltpu.VMEM((offsets, pairs, L), jnp.float32),
            pltpu.VMEM((3, ROWS, bins), jnp.float32),
            dma,
            dma,
            dma((shards,)),
            dma((shards,)),
            dma((shards,)),
            dma((shards,)),
            dma((offsets - 1, shards)),
            dma((offsets - 1, shards)),
        ],
        compiler_params=pltpu.CompilerParams(
            collective_id=0, has_side_effects=True, vmem_limit_bytes=48 * 1024 * 1024
        ),
    )(spectra, pair_mask.T, table)


def solution(mesh):
    return jax.shard_map(
        functools.partial(body, mesh.shape["row"], mesh.shape["col"]),
        mesh=mesh,
        in_specs=(P(None, None, ("grp", "col"), "row"), P("grp", "col")),
        out_specs=P("row", None, ("grp", "col"), None),
        check_vma=False,
    )
```

```python
import functools
import math

import jax
import jax.numpy as jnp
import numpy as np
from jax import lax
from jax.experimental import pallas as pl
from jax.experimental.pallas import tpu as pltpu
from jax.sharding import PartitionSpec as P

WIN = 8
F = 2048
L = 1024
NFFT = 65536
LO_BIN = 2048
GROUP = 8
ROWS = WIN * GROUP
LANES = 128
MESH = pl.DeviceIdType.MESH


def lag_tables(shards):
    bins = LO_BIN + np.arange(F, dtype=np.int32)
    lags = np.arange(L, dtype=np.int32) - L // 2
    turns = np.mod(bins[:, None] * lags[None, :], NFFT).astype(np.float32)
    phase = (turns * np.float32(2.0 * math.pi / NFFT)).astype(np.float64)
    parts = [
        part.astype(np.float32).astype(jnp.bfloat16).reshape(shards, F // shards, L)
        for part in (np.cos(phase), -np.sin(phase))
    ]
    return np.concatenate(parts, axis=1)


def xor(index, mask):
    result = index
    bit = 1
    while bit <= mask:
        if mask & bit:
            result = result + bit - 2 * bit * lax.rem(lax.div(index, bit), 2)
        bit *= 2
    return result


def schedule(shards, offsets):
    far = range(2, shards)
    events = [("T", 0, 1), ("X", 0, 0), ("T", 0, 2), ("O", 1), ("X", 0, 1)]
    events += [("T", 0, m) for m in far if m > 2]
    events += [("T", 1, 0), ("X", 1, 0), ("T", 1, 1), ("X", 1, 1)]
    events += [("T", 1, m) for m in far]
    events += [("T", 2, 0), ("X", 2, 0), ("T", 2, 1), ("O", 2), ("X", 2, 1), ("O", 3), ("X", 0, 2)]
    events += [("T", 2, 2), ("X", 0, 3), ("X", 1, 2), ("T", 2, 3), ("X", 1, 3), ("T", 3, 0), ("X", 2, 2)]
    events += [("X", 2, 3), ("T", 3, 1), ("X", 3, 0), ("T", 3, 2), ("X", 3, 1), ("X", 3, 2)]
    events += [("T", 3, 3), ("X", 3, 3)]
    for m in range(4, shards):
        events += [("O", m), ("T", 2, m), ("T", 3, m)]
        events += [("X", k, m) for k in range(offsets)]
    return events


def kernel(
    shards, blocks, offsets, spectra_hbm, mask, table_hbm, out,
    spectra, owner, partner, table, products, total, sums,
    spectra_sem, table_sem, o_send, o_recv, t_send, t_recv, z_send, z_recv,
):
    me = lax.axis_index("row")
    block = lax.axis_index("col")
    bins = spectra.shape[3]
    groups = owner.shape[1]
    mine = groups * GROUP // shards
    left = lax.rem(block + blocks - 1, blocks)
    right = lax.rem(block + 1, blocks)

    load = pltpu.make_async_copy(table_hbm, table, table_sem)
    fetch = pltpu.make_async_copy(spectra_hbm, spectra, spectra_sem)
    fetch.start()

    barrier = pltpu.get_barrier_semaphore()
    for m in range(1, shards):
        pl.semaphore_signal(barrier, inc=1, device_id={"row": xor(me, m)}, device_id_type=MESH)

    @pl.when(block > 0)
    def _():
        pl.semaphore_signal(barrier, inc=1, device_id={"col": left}, device_id_type=MESH)

    @pl.when(block < blocks - 1)
    def _():
        pl.semaphore_signal(barrier, inc=1, device_id={"col": right}, device_id_type=MESH)

    def whiten(step, carry):
        lanes = pl.ds(pl.multiple_of(step * LANES, LANES), LANES)
        for pair in range(WIN // 2):
            parts = []
            for w in (2 * pair, 2 * pair + 1):
                re = spectra[0, w, :, lanes].astype(jnp.float32)
                im = spectra[1, w, :, lanes].astype(jnp.float32)
                denom = jnp.maximum(jnp.sqrt(re * re + im * im), 0.5)
                parts.append((re / denom, im / denom))
            for c in range(2):
                for g in range(groups):
                    rows = slice(g * GROUP, (g + 1) * GROUP)
                    both = jnp.concatenate([parts[0][c][rows], parts[1][c][rows]], axis=0)
                    owner[0, g, pl.ds(c * ROWS + pair * 2 * GROUP, 2 * GROUP), lanes] = both.astype(jnp.bfloat16)
        return carry

    fetch.wait()
    load.start()
    lax.fori_loop(0, bins // LANES, whiten, 0)

    def group_of(row):
        return lax.div(row * mine, GROUP)

    partner[0, 0] = owner[0, group_of(me)]

    inner = (block > 0).astype(jnp.int32) + (block < blocks - 1).astype(jnp.int32)
    pl.semaphore_wait(barrier, inner + (shards - 1))

    def z_copy(k, m):
        return pltpu.make_async_remote_copy(
            src_ref=partner.at[k - 1, m], dst_ref=partner.at[k, m],
            send_sem=z_send.at[k - 1, m], recv_sem=z_recv.at[k - 1, m],
            device_id={"col": left}, device_id_type=MESH,
        )

    def t_copy(m):
        peer = xor(me, m)
        return pltpu.make_async_remote_copy(
            src_ref=owner.at[0, group_of(peer)], dst_ref=partner.at[0, m],
            send_sem=t_send.at[m], recv_sem=t_recv.at[m],
            device_id={"row": peer}, device_id_type=MESH,
        )

    def o_copy(m):
        relayed = m % 2 == 1 and m > 1
        return pltpu.make_async_remote_copy(
            src_ref=owner.at[m - 1 if relayed else 0], dst_ref=owner.at[m],
            send_sem=o_send.at[m], recv_sem=o_recv.at[m],
            device_id={"row": xor(me, 1 if relayed else m)}, device_id_type=MESH,
        )

    def forward(k, m):
        if k < offsets:
            @pl.when((block > 0) & (block + k - 1 < blocks))
            def _():
                z_copy(k, m).start()

    forward(1, 0)
    for m in range(1, shards):
        t_copy(m).start()
    o_copy(1).start()
    for m in range(2, shards, 2):
        o_copy(m).start()
    load.wait()

    first_row = lax.rem(me * mine, GROUP) if mine < GROUP else 0

    steps = bins // LANES
    wide = L // groups

    def prepare(k, m):
        re = partner[k, m, :ROWS, :].astype(jnp.float32)
        im = partner[k, m, ROWS:, :].astype(jnp.float32)
        for number, rows in enumerate((re, re + im, im - re)):
            kept = rows
            for offset in range(mine, GROUP, mine):
                moved = jnp.concatenate([rows[offset:], rows[:offset]], axis=0)
                kept = jnp.where(first_row == offset, moved, kept)
            sums[number] = kept

    def cross(m, slot, g, step):
        lanes = pl.ds(step * LANES, LANES)
        a = owner[m, g, :ROWS, lanes].astype(jnp.float32)
        b = owner[m, g, ROWS:, lanes].astype(jnp.float32)
        a = [a[w * GROUP:(w + 1) * GROUP] for w in range(WIN)]
        b = [b[w * GROUP:(w + 1) * GROUP] for w in range(WIN)]
        p = [x - y for x, y in zip(a, b)]
        for pair in range(mine // 2):
            reals, imags = [], []
            for j in (2 * pair, 2 * pair + 1):
                s = [None, None, None]
                for w in range(WIN):
                    row = pl.ds(w * GROUP + j, 1)
                    terms = (
                        p[w] * sums[0, row, lanes],
                        b[w] * sums[1, row, lanes],
                        a[w] * sums[2, row, lanes],
                    )
                    s = [t if x is None else x + t for x, t in zip(s, terms)]
                reals.append(s[0] + s[1])
                imags.append(s[0] + s[2])
            rows = pl.ds(pl.multiple_of(g * (mine * GROUP) + pair * 2 * GROUP, 2 * GROUP), 2 * GROUP)
            products[slot, rows, lanes] = jnp.concatenate(reals, axis=0).astype(jnp.bfloat16)
            products[slot, rows, pl.ds(bins + step * LANES, LANES)] = jnp.concatenate(imags, axis=0).astype(jnp.bfloat16)

    def lags(k, m, slot, g):
        columns = pl.ds(pl.multiple_of(g * wide, wide), wide)
        part = jnp.dot(products[slot], table[xor(me, m), :, columns], preferred_element_type=jnp.float32)
        if m > 0:
            part = part + total[k, :, columns]
        total[k, :, columns] = part

    def work(task, earlier):
        if task:
            prepare(*task[:2])

        def one(g, carry):
            if earlier:
                lags(*earlier, g)
            if task:
                for step in range(steps):
                    cross(task[1], task[2], g, step)
            return carry

        lax.fori_loop(0, groups, one, 0)
        if earlier and earlier[1] == shards - 1:
            finish(earlier[0])

    def finish(k):
        factor = mask[0, k].astype(jnp.float32) * (1.0 / math.sqrt(F * WIN))
        for j in range(mine):
            for g in range(0, groups, 2):
                pieces = [total[k, pl.ds(((g + s) * mine + j) * GROUP, GROUP), :] for s in range(2)]
                both = jnp.concatenate(pieces, axis=0) * factor
                out[j, k, pl.ds(g * GROUP, 2 * GROUP), :] = both.astype(out.dtype)

    def active(k):
        return block + k < blocks

    for k in range(1, offsets):
        @pl.when(block + k >= blocks)
        def _(k=k):
            out[:, k] = jnp.zeros((mine, groups * GROUP, L), out.dtype)

    pending, slot = None, 0
    for event in schedule(shards, offsets):
        if event[0] == "O":
            m = event[1]
            o_copy(m).wait_recv()
            if m % 2 == 0:
                o_copy(m + 1).start()
        elif event[0] == "T":
            k, m = event[1:]
            if k == 0:
                t_copy(m).wait_recv()
            else:
                @pl.when(block + k < blocks)
                def _(k=k, m=m):
                    z_copy(k, m).wait_recv()
            forward(k + 1, m)
        else:
            task = event[1:] + (slot,)
            k = task[0]
            older = pending[0] if pending else k

            @pl.when(active(max(k, older)))
            def _(task=task, pending=pending):
                work(task, pending)

            if older < k:
                @pl.when(active(older) & (block + k >= blocks))
                def _(pending=pending):
                    work(None, pending)

            if older > k:
                @pl.when(active(k) & (block + older >= blocks))
                def _(task=task):
                    work(task, None)

            pending, slot = task, 1 - slot

    @pl.when(active(pending[0]))
    def _():
        work(None, pending)

    for m in range(1, shards):
        t_copy(m).wait_send()
        o_copy(m).wait_send()
    for k in range(1, offsets):
        @pl.when((block > 0) & (block + k - 1 < blocks))
        def _(k=k):
            for m in range(shards):
                z_copy(k, m).wait_send()


def body(shards, blocks, spectra, pair_mask):
    channels, bins = spectra.shape[2:]
    offsets = pair_mask.shape[0]
    groups = channels // GROUP
    mine = channels // shards
    table = lag_tables(shards)
    chunk = (2 * ROWS, bins)
    pairs = mine * channels
    dma = pltpu.SemaphoreType.DMA
    return pl.pallas_call(
        functools.partial(kernel, shards, blocks, offsets),
        out_shape=jax.ShapeDtypeStruct((mine, offsets, channels, L), jnp.bfloat16),
        in_specs=[
            pl.BlockSpec(memory_space=pl.ANY),
            pl.BlockSpec(memory_space=pltpu.SMEM),
            pl.BlockSpec(memory_space=pl.ANY),
        ],
        out_specs=pl.BlockSpec(memory_space=pltpu.VMEM),
        scratch_shapes=[
            pltpu.VMEM(spectra.shape, jnp.bfloat16),
            pltpu.VMEM((shards, groups) + chunk, jnp.bfloat16),
            pltpu.VMEM((offsets, shards) + chunk, jnp.bfloat16),
            pltpu.VMEM(table.shape, jnp.bfloat16),
            pltpu.VMEM((2, pairs, 2 * bins), jnp.bfloat16),
            pltpu.VMEM((offsets, pairs, L), jnp.float32),
            pltpu.VMEM((3, ROWS, bins), jnp.float32),
            dma,
            dma,
            dma((shards,)),
            dma((shards,)),
            dma((shards,)),
            dma((shards,)),
            dma((offsets - 1, shards)),
            dma((offsets - 1, shards)),
        ],
        compiler_params=pltpu.CompilerParams(
            collective_id=0, has_side_effects=True, vmem_limit_bytes=48 * 1024 * 1024
        ),
    )(spectra, pair_mask.T, table)


def solution(mesh):
    return jax.shard_map(
        functools.partial(body, mesh.shape["row"], mesh.shape["col"]),
        mesh=mesh,
        in_specs=(P(None, None, ("grp", "col"), "row"), P("grp", "col")),
        out_specs=P("row", None, ("grp", "col"), None),
        check_vma=False,
    )
```
